32 devices in a mesh: groups: 2 (over x), blk: 16 (over z, y, core).
Axes of the slice: x: 2, y: 2, z: 4, core: 2. Of those that a mesh axis runs over, the one named last changes fastest.
Arguments:
- queries: bfloat16 [32768, 1024], P(('groups', 'blk')), parts along dimension 0, may hold values from -2.5 to 2.5
- passages: bfloat16 [128, 256, 1024], P('blk', 'groups'), parts along dimension 1, may hold values from -12 to 12
- block_list: int32 [256, 4], P(('groups', 'blk')), parts along dimension 0, may hold values from 0 to 127, as said below
- pair_count: int32 [256], P(('groups', 'blk')), parts along dimension 0, may hold values from 1 to 4, 256 in all
- positive: int32 [32768], P(('groups', 'blk')), parts along dimension 0, may hold values from 0 to 511
Outputs:
- row_loss: float32 [32768], P(('groups', 'blk')), parts along dimension 0
- query_grad: bfloat16 [32768, 1024], P(('groups', 'blk')), parts along dimension 0
- passage_grad: bfloat16 [128, 256, 1024], P('blk', 'groups'), parts along dimension 1
The draws below stay inside these ranges and needn't reach their ends.
There are 2 independent parts, one for each index of `groups`. The reference program is written for one: setup_inputs(seed, part) draws one part's arguments, and reference() takes and returns one part's arrays. A program takes and returns all parts, laid end to end along the dimension named above; each array names one. Nothing has to cross between parts.
Inputs may be any that keep to these rules, and one draw needn't show every extreme that they name: `block_list`: each row names 4 different passage blocks; the 8 rows of one index of blk (aligned runs of 8 rows) name exactly 8 different passage blocks in all, each of them in the same number of rows. `pair_count`: the 128 entries of one group sum to 256, and some entry of each group equals 4; the sum holds for each group separately, not over all groups together.
All inputs are finite; a program needn't handle non-finite values.
Results may differ from the reference program's by a relative error of at most 0.0039.
Values may be sent and summed in bfloat16 or wider, within the bound.
A program may use at most 128 MiB of HBM per device.

```python
import math
import jax
import jax.numpy as jnp
import numpy as np
from jax import lax

D = 1024
BLK = 128
NB = 4
QB_DEV = 8
DISTINCT = 8
QBLOCKS = 128
PBLOCKS = 128
NQ = 16384


def draw_queries(key, part):
    noise_key = jax.random.fold_in(jax.random.fold_in(key, 11), 0)
    values_q = 0.1 * jnp.clip(jax.random.normal(noise_key, (NQ, D), jnp.float32), -6.0, 6.0)
    return jnp.clip(values_q, -2.5, 2.5).astype(jnp.bfloat16)


def draw_passages(key, part):
    noise_key = jax.random.fold_in(jax.random.fold_in(key, 13), 0)
    noise_part = jnp.clip(jax.random.normal(noise_key, (BLK, PBLOCKS, D), jnp.float32), -6.0, 6.0)
    return jnp.clip(noise_part, -12.0, 12.0).astype(jnp.bfloat16)


def draw_block_list(key, part):
    holders = QBLOCKS // QB_DEV
    device_keys = jax.random.split(jax.random.fold_in(key, 17), holders)

    def one_device(device_key):
        pool_key, order_key = jax.random.split(device_key)
        pool = jax.random.permutation(pool_key, PBLOCKS)[:DISTINCT]
        quarter_keys = jax.random.split(order_key, 4)
        orders = jnp.stack([jax.random.permutation(quarter_keys[index], DISTINCT) for index in range(4)])
        return pool[orders.reshape(-1)].reshape(QB_DEV, NB)
    return jax.vmap(one_device)(device_keys).reshape(QBLOCKS, NB).astype(jnp.int32)


def set_ends(array, stream_key, low, largest):
    place = [jax.random.randint(jax.random.fold_in(stream_key, axis), (), 0, length) for axis, length in enumerate(array.shape)]
    widest = array.shape.index(max(array.shape))
    next_to = place[:widest] + [(place[widest] + 1) % array.shape[widest]] + place[widest + 1:]
    return array.at[tuple(place)].set(low).at[tuple(next_to)].set(largest)


def split_up(amount, total, reach, skew):
    weights = [(1 << 20) // math.isqrt(grade ** skew) + 1 for grade in range(2, amount + 1)]
    rest, holding = total - reach - (amount - 1), [1] * (amount - 1)
    while rest > 0:
        free = [i for i in range(amount - 1) if holding[i] < reach]
        whole, left = sum([weights[i] for i in free]), rest
        for i in free:
            extra = min(reach - holding[i], max(1, left * weights[i] // whole), rest)
            holding[i] = holding[i] + extra
            rest = rest - extra
    return np.array([reach] + holding)


def uneven_parts(rng, amount, total, bound, slope):
    if amount == 2:
        one = jax.random.randint(rng, (), max(1, total - bound), min(bound, total - 1) + 1)
        return jnp.stack([one, total - one])
    tallies = jnp.asarray(split_up(amount, total, bound, slope), jnp.int32)
    pairs = (amount - 1) // 2
    source_of, receiver = tallies[1:1 + 2 * pairs:2], tallies[2:2 + 2 * pairs:2]
    margin = jnp.minimum(source_of - 1, bound - receiver)
    passed = jax.random.randint(jax.random.fold_in(rng, 1), (pairs,), 0, 1 << 20) % (margin + 1)
    tallies = tallies.at[1:1 + 2 * pairs:2].set(source_of - passed).at[2:2 + 2 * pairs:2].set(receiver + passed)
    return tallies[jax.random.permutation(jax.random.fold_in(rng, 2), amount)]


def setup_inputs(seed: int = 0, part: int = 0) -> dict:
    keys = jax.random.split(jax.random.key(seed), 6)
    part_keys = jax.random.split(jax.random.fold_in(keys[5], part), 6)
    queries = draw_queries(jax.random.fold_in(jax.random.fold_in(keys[5], part), 71), part)
    passages = draw_passages(jax.random.fold_in(jax.random.fold_in(keys[5], part), 71), part)
    block_list = draw_block_list(jax.random.fold_in(jax.random.fold_in(keys[5], part), 71), part)
    pair_count = uneven_parts(part_keys[3], QBLOCKS, QBLOCKS * NB // 2, NB, 2).astype(jnp.int32)
    positive = set_ends(jax.random.randint(part_keys[4], (NQ,), 0, NB * BLK), jax.random.fold_in(part_keys[4], 1), 0, (NB * BLK) - 1).astype(jnp.int32)
    return {"queries": queries, "passages": passages, "block_list": block_list, "pair_count": pair_count, "positive": positive}


def reference(queries, passages, block_list, pair_count, positive):
    passage_blocks = jnp.transpose(passages, (1, 0, 2))
    query_blocks = queries.reshape(QBLOCKS, BLK, D)
    targets = positive.reshape(QBLOCKS, BLK)
    span_cols = NB * BLK

    def visit_block(grad_total, inputs):
        query_rows, block_ids, live_count, slot_raw = inputs
        candidates = passage_blocks[block_ids].reshape(span_cols, D)
        scores = jnp.dot(query_rows, candidates.T, preferred_element_type=jnp.float32)
        columns = jnp.arange(span_cols, dtype=jnp.int32)
        live_limit = live_count * BLK
        is_live = columns[None, :] < live_limit
        target_slot = slot_raw % live_limit
        row_max = jnp.max(jnp.where(is_live, scores, -jnp.inf), axis=1, keepdims=True)
        weights = jnp.where(is_live, jnp.exp(scores - row_max), jnp.float32(0.0))
        row_sum = jnp.sum(weights, axis=1, keepdims=True)
        target = jnp.take_along_axis(scores, target_slot[:, None], axis=1)[:, 0]
        row_loss = row_max[:, 0] + jnp.log(row_sum[:, 0]) - target
        onehot = (columns[None, :] == target_slot[:, None]).astype(jnp.float32)
        grad_scores = (weights / row_sum - onehot).astype(jnp.bfloat16)
        query_grad = jnp.dot(grad_scores, candidates, preferred_element_type=jnp.float32).astype(jnp.bfloat16)
        contrib = jnp.dot(grad_scores.T, query_rows, preferred_element_type=jnp.float32).reshape(NB, BLK, D)
        grad_total = grad_total.at[block_ids].add(contrib)
        return grad_total, (row_loss, query_grad)

    start_total = jnp.zeros((PBLOCKS, BLK, D), jnp.float32)
    grad_total, (row_loss, query_grad) = lax.scan(visit_block, start_total, (query_blocks, block_list, pair_count, targets))
    passage_grad = jnp.transpose(grad_total, (1, 0, 2)).astype(jnp.bfloat16)
    return row_loss.reshape(NQ), query_grad.reshape(NQ, D), passage_grad
```

```python
import functools
import jax
import jax.numpy as jnp
from jax import lax
from jax.experimental import pallas as pl
from jax.experimental.pallas import tpu as pltpu
from jax.sharding import PartitionSpec as P

BLK = 128
NB = 4
DISTINCT = 8
F32 = jnp.float32
BF16 = jnp.bfloat16
NT = (((1,), (1,)), ((), ()))
TN = (((0,), (0,)), ((), ()))
TILE = 256
FAR = 3.0e38


def dot(a, b, dims=(((1,), (0,)), ((), ()))):
    return lax.dot_general(a, b, dims, preferred_element_type=F32)


def tiles(length, step):
    def over(body):
        def one(i, carry):
            body(pl.ds(pl.multiple_of(i * step, step), step))
            return carry

        lax.fori_loop(0, length // step, one, 0)

    return over


def kernel(
    n,
    q_hbm, p_hbm, bl, pc, pos,
    loss, qg_hbm, pg_hbm,
    q, p, wsend, wrecv, hot, send, recv, s, g, rsend, rrecv, acc, qg, pg, live, tgt, m8, t8,
    in_sem, own_sem, out_sem, w_s, w_r, f_s, f_r, r_s, r_r,
):
    rows, width = q.shape
    held = p.shape[0]
    pb = wsend.shape[1]
    r_here = held // pb
    mrows = r_here * DISTINCT
    qblocks = rows // BLK
    per = max(1, TILE // mrows)
    groups = list(reversed(range(n // per)))
    me = lax.axis_index("blk")

    def peer(x):
        out, bit = me, 1
        while bit < n:
            if x & bit:
                out = out + bit - 2 * bit * (lax.rem(lax.div(me, bit), 2))
            bit *= 2
        return out

    def remote(src, dst, ss, rs, x):
        return pltpu.make_async_remote_copy(
            src_ref=src, dst_ref=dst, send_sem=ss.at[x], recv_sem=rs.at[x],
            device_id={"blk": peer(x)}, device_id_type=pl.DeviceIdType.MESH,
        )

    def slot(ref, x):
        return ref.at[pl.ds(x * mrows, mrows)]

    def members(grp):
        return [x for x in range(grp * per, (grp + 1) * per)]

    def w_copy(x):
        return remote(wsend, wrecv.at[pl.ds(x * DISTINCT, DISTINCT)], w_s, w_r, x)

    def f_copy(x):
        return remote(slot(send, x), slot(recv, x), f_s, f_r, x)

    def r_copy(x):
        return remote(slot(rsend, x), slot(rrecv, x), r_s, r_r, x)

    load_q = pltpu.make_async_copy(q_hbm, q, in_sem.at[0])
    load_p = pltpu.make_async_copy(p_hbm, p, in_sem.at[1])
    load_p.start()
    load_q.start()
    barrier = pltpu.get_barrier_semaphore()
    for x in range(1, n):
        pl.semaphore_signal(barrier, inc=1, device_id={"blk": peer(x)}, device_id_type=pl.DeviceIdType.MESH)

    lane = lax.broadcasted_iota(jnp.int32, (DISTINCT, pb), 1)
    sub = lax.broadcasted_iota(jnp.int32, (DISTINCT, pb), 0)
    named = lane < 0
    for k in range(qblocks):
        for j in range(NB):
            named = named | (lane == bl[k, j])
    named = named.astype(F32)
    before = (
        lax.broadcasted_iota(jnp.int32, (pb, pb), 0) < lax.broadcasted_iota(jnp.int32, (pb, pb), 1)
    ).astype(F32).astype(BF16)
    rank = dot(named.astype(BF16), before)
    mine = jnp.where(rank == sub.astype(F32), named, 0.0)
    wsend[...] = mine
    wrecv[pl.ds(0, DISTINCT), :] = mine

    pl.semaphore_wait(barrier, n - 1)
    for grp in groups:
        for x in members(grp):
            if x:
                w_copy(x).start()

    wanted = jnp.sum(mine * lane.astype(F32), axis=1, keepdims=True).astype(jnp.int32)
    for k in range(qblocks):
        at = pl.ds(k * BLK, BLK)
        place = jnp.broadcast_to(pos[pl.ds(k, 1), :], (DISTINCT, BLK))
        count = pc[k]
        nth = lax.shift_right_logical(place, 7)
        for _ in range(NB - 1):
            nth = jnp.where(nth >= count, nth - count, nth)
        row = place & (BLK - 1)
        is_live = jnp.zeros((DISTINCT, BLK), F32)
        target = jnp.full((DISTINCT, BLK), -1, jnp.int32)
        for j in range(NB):
            here = jnp.broadcast_to(wanted, (DISTINCT, BLK)) == bl[k, j]
            is_live = jnp.where(here & (jnp.full((DISTINCT, BLK), j, jnp.int32) < count), 1.0, is_live)
            target = jnp.where(here & (nth == j), row, target)
        live[:, at] = is_live
        tgt[:, at] = target

    load_p.wait()
    wide = lax.broadcasted_iota(jnp.int32, (DISTINCT, held), 1)
    for grp in groups:
        for x in members(grp):
            if x:
                w_copy(x).wait_recv()
            w = wrecv[pl.ds(x * DISTINCT, DISTINCT), :]
            w = jnp.concatenate([w] * r_here, axis=1)
            parts = [
                jnp.where((wide >= r * pb) & (wide < (r + 1) * pb), w, 0.0) for r in range(r_here)
            ]
            hot[pl.ds(x * mrows, mrows), :] = jnp.concatenate(parts, axis=0).astype(BF16)
        at = pl.ds(grp * per * mrows, per * mrows)

        @tiles(width, TILE)
        def _(col):
            send[at, col] = dot(hot[at, :], p[:, col]).astype(BF16)

        for x in members(grp):
            if x:
                f_copy(x).start()
    own = pltpu.make_async_copy(slot(send, 0), slot(recv, 0), own_sem)
    own.start()
    load_q.wait()

    m8[...] = jnp.full(m8.shape, -FAR, F32)
    t8[...] = jnp.zeros(t8.shape, F32)
    for grp in groups:
        for x in members(grp):
            if x:
                f_copy(x).wait_recv()
            else:
                own.wait()
        at = pl.ds(grp * per * mrows, per * mrows)

        @tiles(rows, TILE)
        def _(col):
            part = dot(recv[at, :], q[col, :], NT)
            s[at, col] = part
            cube = part.reshape(per * r_here, DISTINCT, TILE)
            m8[:, col] = jnp.maximum(m8[:, col], jnp.max(cube, axis=0))
            total = t8[:, col]
            want = tgt[:, col]
            for i, x in enumerate(members(grp)):
                base = peer(x) * r_here
                for r in range(r_here):
                    total = total + jnp.where(want == base + r, cube[i * r_here + r], 0.0)
            t8[:, col] = total

    shown = live[...] > 0.0
    top = jnp.max(jnp.where(shown, m8[...], -FAR), axis=0, keepdims=True)
    shift = jnp.where(shown, top, FAR)
    m8[...] = shift

    def weigh(i, total):
        at = pl.ds(pl.multiple_of(i * 64, 64), 64)
        cube = s[at, :].reshape(64 // DISTINCT, DISTINCT, rows)
        e = jnp.exp(cube - m8[...][None])
        s[at, :] = e.reshape(64, rows)
        return total + jnp.sum(e, axis=0)

    total = lax.fori_loop(0, n * mrows // 64, weigh, jnp.zeros((DISTINCT, rows), F32))
    row_sum = jnp.sum(total, axis=0, keepdims=True)
    value = top + jnp.log(row_sum) - jnp.sum(t8[...], axis=0, keepdims=True)
    for k in range(qblocks):
        loss[pl.ds(k, 1), :] = value[:, k * BLK:(k + 1) * BLK]
    t8[...] = jnp.broadcast_to(1.0 / row_sum, t8.shape)

    for grp in groups:
        for x in members(grp):
            base = peer(x) * r_here
            at = pl.ds(x * mrows, mrows)
            cube = s[at, :].reshape(r_here, DISTINCT, rows)
            which = base + lax.broadcasted_iota(jnp.int32, cube.shape, 0)
            one = jnp.where(tgt[...][None] == which, 1.0, 0.0)
            g[at, :] = (cube * t8[...][None] - one).reshape(mrows, rows).astype(BF16)
        at = pl.ds(grp * per * mrows, per * mrows)

        @tiles(width, TILE)
        def _(col):
            rsend[at, col] = dot(g[at, :], q[:, col]).astype(BF16)

        for x in members(grp):
            if x:
                r_copy(x).start()

    @tiles(width, TILE)
    def _(col):
        qg[:, col] = dot(g[...], recv[:, col], TN).astype(BF16)

    store_qg = pltpu.make_async_copy(qg, qg_hbm, out_sem.at[0])
    store_qg.start()

    own = pltpu.make_async_copy(slot(rsend, 0), slot(rrecv, 0), own_sem)
    own.start()
    for grp in groups:
        for x in members(grp):
            if x:
                r_copy(x).wait_recv()
            else:
                own.wait()
        at = pl.ds(grp * per * mrows, per * mrows)

        @tiles(width, TILE)
        def _(col):
            part = dot(hot[at, :], rrecv[at, col], TN)
            if grp != groups[0]:
                part = part + acc[:, col]
            if grp == groups[-1]:
                pg[:, col] = part.astype(BF16)
            else:
                acc[:, col] = part

    store_pg = pltpu.make_async_copy(pg, pg_hbm, out_sem.at[1])
    store_pg.start()
    for x in range(1, n):
        w_copy(x).wait_send()
        f_copy(x).wait_send()
        r_copy(x).wait_send()
    store_qg.wait()
    store_pg.wait()


def body(n, queries, passages, block_list, pair_count, positive):
    rows, width = queries.shape
    r_here, pb, _ = passages.shape
    held = r_here * pb
    total = n * r_here * DISTINCT
    any_space = pl.BlockSpec(memory_space=pl.ANY)
    smem = pl.BlockSpec(memory_space=pltpu.SMEM)
    vmem = pl.BlockSpec(memory_space=pltpu.VMEM)
    dma = pltpu.SemaphoreType.DMA
    loss, query_grad, passage_grad = pl.pallas_call(
        functools.partial(kernel, n),
        out_shape=(
            jax.ShapeDtypeStruct((rows // BLK, BLK), F32),
            jax.ShapeDtypeStruct((rows, width), BF16),
            jax.ShapeDtypeStruct((held, width), BF16),
        ),
        in_specs=[any_space, any_space, smem, smem, vmem],
        out_specs=(vmem, any_space, any_space),
        scratch_shapes=[
            pltpu.VMEM((rows, width), BF16),
            pltpu.VMEM((held, width), BF16),
            pltpu.VMEM((DISTINCT, pb), F32),
            pltpu.VMEM((n * DISTINCT, pb), F32),
            pltpu.VMEM((total, held), BF16),
            pltpu.VMEM((total, width), BF16),
            pltpu.VMEM((total, width), BF16),
            pltpu.VMEM((total, rows), F32),
            pltpu.VMEM((total, rows), BF16),
            pltpu.VMEM((total, width), BF16),
            pltpu.VMEM((total, width), BF16),
            pltpu.VMEM((held, width), F32),
            pltpu.VMEM((rows, width), BF16),
            pltpu.VMEM((held, width), BF16),
            pltpu.VMEM((DISTINCT, rows), F32),
            pltpu.VMEM((DISTINCT, rows), jnp.int32),
            pltpu.VMEM((DISTINCT, rows), F32),
            pltpu.VMEM((DISTINCT, rows), F32),
            dma((2,)),
            dma,
            dma((2,)),
            dma((n,)), dma((n,)), dma((n,)), dma((n,)), dma((n,)), dma((n,)),
        ],
        compiler_params=pltpu.CompilerParams(
            collective_id=0, has_side_effects=True, vmem_limit_bytes=52 * 1024 * 1024
        ),
        cost_estimate=pl.CostEstimate(
            flops=10 * rows * width * total, bytes_accessed=8 * rows * width, transcendentals=total * rows
        ),
    )(
        queries,
        passages.reshape(held, width),
        block_list,
        pair_count,
        positive.reshape(rows // BLK, BLK),
    )
    return loss.reshape(-1), query_grad, passage_grad.reshape(passages.shape)


def solution(mesh):
    return jax.shard_map(
        functools.partial(body, mesh.shape["blk"]),
        mesh=mesh,
        in_specs=(
            P(("groups", "blk"), None),
            P("blk", "groups", None),
            P(("groups", "blk"), None),
            P(("groups", "blk")),
            P(("groups", "blk")),
        ),
        out_specs=(P(("groups", "blk")), P(("groups", "blk"), None), P("blk", "groups", None)),
        check_vma=False,
    )
```

```python
import functools
import jax
import jax.numpy as jnp
from jax import lax
from jax.experimental import pallas as pl
from jax.experimental.pallas import tpu as pltpu
from jax.sharding import PartitionSpec as P

BLK = 128
NB = 4
DISTINCT = 8
F32 = jnp.float32
BF16 = jnp.bfloat16
NT = (((1,), (1,)), ((), ()))
TN = (((0,), (0,)), ((), ()))
TILE = 256
FAR = 3.0e38


def dot(a, b, dims=(((1,), (0,)), ((), ()))):
    return lax.dot_general(a, b, dims, preferred_element_type=F32)


def tiles(length, step):
    def over(body):
        def one(i, carry):
            body(pl.ds(pl.multiple_of(i * step, step), step))
            return carry

        lax.fori_loop(0, length // step, one, 0)

    return over


def kernel(
    n,
    q_hbm, p_hbm, bl_hbm, pc_hbm, pos_hbm,
    loss, qg, pg,
    q, p, bl, pc, pos, wsend, wrecv, hot, send, recv, s, g, rsend, rrecv, acc, live, tgt, m8, t8,
    in_sem, own_sem, w_s, w_r, f_s, f_r, r_s, r_r,
):
    rows, width = q.shape
    held = p.shape[0]
    pb = wsend.shape[1]
    r_here = held // pb
    mrows = r_here * DISTINCT
    qblocks = rows // BLK
    per = max(1, TILE // mrows)
    groups = list(range(n // per))
    half = n // 2
    order = [x for i in range(half) for x in (half + i, (i + 1) % half)]
    place_of = {x: i for i, x in enumerate(order)}
    me = lax.axis_index("blk")

    def peer(x):
        out, bit = me, 1
        while bit < n:
            if x & bit:
                out = out + bit - 2 * bit * (lax.rem(lax.div(me, bit), 2))
            bit *= 2
        return out

    def remote(src, dst, ss, rs, x):
        return pltpu.make_async_remote_copy(
            src_ref=src, dst_ref=dst, send_sem=ss.at[x], recv_sem=rs.at[x],
            device_id={"blk": peer(x)}, device_id_type=pl.DeviceIdType.MESH,
        )

    def slot(ref, x):
        return ref.at[pl.ds(place_of[x] * mrows, mrows)]

    def members(grp):
        return order[grp * per:(grp + 1) * per]

    def w_copy(x):
        return remote(wsend, wrecv.at[pl.ds(x * DISTINCT, DISTINCT)], w_s, w_r, x)

    def f_copy(x):
        return remote(slot(send, x), slot(recv, x), f_s, f_r, x)

    def r_copy(x):
        return remote(slot(rsend, x), slot(rrecv, x), r_s, r_r, x)

    load_q = pltpu.make_async_copy(q_hbm, q, in_sem.at[0])
    load_p = pltpu.make_async_copy(p_hbm, p, in_sem.at[1])
    small = [
        pltpu.make_async_copy(a, b, in_sem.at[2 + i])
        for i, (a, b) in enumerate(((bl_hbm, bl), (pc_hbm, pc), (pos_hbm, pos)))
    ]
    for one in small:
        one.start()
    load_p.start()
    load_q.start()
    barrier = pltpu.get_barrier_semaphore()
    for x in range(1, n):
        pl.semaphore_signal(barrier, inc=1, device_id={"blk": peer(x)}, device_id_type=pl.DeviceIdType.MESH)

    lane = lax.broadcasted_iota(jnp.int32, (DISTINCT, pb), 1)
    sub = lax.broadcasted_iota(jnp.int32, (DISTINCT, pb), 0)
    small[0].wait()
    named = lane < 0
    for k in range(qblocks):
        for j in range(NB):
            named = named | (lane == bl[j, k])
    named = named.astype(F32)
    before = (
        lax.broadcasted_iota(jnp.int32, (pb, pb), 0) < lax.broadcasted_iota(jnp.int32, (pb, pb), 1)
    ).astype(F32).astype(BF16)
    rank = dot(named.astype(BF16), before)
    mine = jnp.where(rank == sub.astype(F32), named, 0.0)
    wsend[...] = mine
    wrecv[pl.ds(0, DISTINCT), :] = mine

    pl.semaphore_wait(barrier, n - 1)
    for grp in groups:
        for x in members(grp):
            if x:
                w_copy(x).start()

    wanted = jnp.sum(mine * lane.astype(F32), axis=1, keepdims=True).astype(jnp.int32)
    small[1].wait()
    small[2].wait()
    for k in range(qblocks):
        at = pl.ds(k * BLK, BLK)
        place = jnp.broadcast_to(pos[pl.ds(k, 1), :], (DISTINCT, BLK))
        count = pc[k]
        nth = lax.shift_right_logical(place, 7)
        for _ in range(NB - 1):
            nth = jnp.where(nth >= count, nth - count, nth)
        row = place & (BLK - 1)
        is_live = jnp.zeros((DISTINCT, BLK), F32)
        target = jnp.full((DISTINCT, BLK), -1, jnp.int32)
        for j in range(NB):
            here = jnp.broadcast_to(wanted, (DISTINCT, BLK)) == bl[j, k]
            is_live = jnp.where(here & (jnp.full((DISTINCT, BLK), j, jnp.int32) < count), 1.0, is_live)
            target = jnp.where(here & (nth == j), row, target)
        live[:, at] = is_live
        tgt[:, at] = target

    load_p.wait()
    wide = lax.broadcasted_iota(jnp.int32, (DISTINCT, held), 1)
    for grp in groups:
        for x in members(grp):
            if x:
                w_copy(x).wait_recv()
            w = wrecv[pl.ds(x * DISTINCT, DISTINCT), :]
            w = jnp.concatenate([w] * r_here, axis=1)
            parts = [
                jnp.where((wide >= r * pb) & (wide < (r + 1) * pb), w, 0.0) for r in range(r_here)
            ]
            hot[pl.ds(place_of[x] * mrows, mrows), :] = jnp.concatenate(parts, axis=0).astype(BF16)
        at = pl.ds(grp * per * mrows, per * mrows)

        @tiles(width, TILE)
        def _(col):
            send[at, col] = dot(hot[at, :], p[:, col]).astype(BF16)

        for x in members(grp):
            if x:
                f_copy(x).start()
    own = pltpu.make_async_copy(slot(send, 0), slot(recv, 0), own_sem)
    own.start()
    load_q.wait()

    m8[...] = jnp.full(m8.shape, -FAR, F32)
    t8[...] = jnp.zeros(t8.shape, F32)
    for grp in groups:
        for x in members(grp):
            if x:
                f_copy(x).wait_recv()
            else:
                own.wait()
        at = pl.ds(grp * per * mrows, per * mrows)

        @tiles(rows, TILE)
        def _(col):
            part = dot(recv[at, :], q[col, :], NT)
            s[at, col] = part
            cube = part.reshape(per * r_here, DISTINCT, TILE)
            m8[:, col] = jnp.maximum(m8[:, col], jnp.max(cube, axis=0))
            total = t8[:, col]
            want = tgt[:, col]
            for i, x in enumerate(members(grp)):
                base = peer(x) * r_here
                for r in range(r_here):
                    total = total + jnp.where(want == base + r, cube[i * r_here + r], 0.0)
            t8[:, col] = total

    shown = live[...] > 0.0
    top = jnp.max(jnp.where(shown, m8[...], -FAR), axis=0, keepdims=True)
    shift = jnp.where(shown, top, FAR)
    m8[...] = shift

    def weigh(i, total):
        at = pl.ds(pl.multiple_of(i * 64, 64), 64)
        cube = s[at, :].reshape(64 // DISTINCT, DISTINCT, rows)
        e = jnp.exp(cube - m8[...][None])
        s[at, :] = e.reshape(64, rows)
        return total + jnp.sum(e, axis=0)

    total = lax.fori_loop(0, n * mrows // 64, weigh, jnp.zeros((DISTINCT, rows), F32))
    row_sum = jnp.sum(total, axis=0, keepdims=True)
    value = top + jnp.log(row_sum) - jnp.sum(t8[...], axis=0, keepdims=True)
    for k in range(qblocks):
        loss[pl.ds(k, 1), :] = value[:, k * BLK:(k + 1) * BLK]
    t8[...] = jnp.broadcast_to(1.0 / row_sum, t8.shape)

    for grp in groups:
        for x in members(grp):
            base = peer(x) * r_here
            at = pl.ds(place_of[x] * mrows, mrows)
            cube = s[at, :].reshape(r_here, DISTINCT, rows)
            which = base + lax.broadcasted_iota(jnp.int32, cube.shape, 0)
            one = jnp.where(tgt[...][None] == which, 1.0, 0.0)
            g[at, :] = (cube * t8[...][None] - one).reshape(mrows, rows).astype(BF16)
        at = pl.ds(grp * per * mrows, per * mrows)

        @tiles(width, TILE)
        def _(col):
            rsend[at, col] = dot(g[at, :], q[:, col]).astype(BF16)

        for x in members(grp):
            if x:
                r_copy(x).start()

    @tiles(width, TILE)
    def _(col):
        qg[:, col] = dot(g[...], recv[:, col], TN).astype(BF16)


    own = pltpu.make_async_copy(slot(rsend, 0), slot(rrecv, 0), own_sem)
    own.start()
    for grp in groups:
        for x in members(grp):
            if x:
                r_copy(x).wait_recv()
            else:
                own.wait()
        at = pl.ds(grp * per * mrows, per * mrows)

        @tiles(width, TILE)
        def _(col):
            part = dot(hot[at, :], rrecv[at, col], TN)
            if grp != groups[0]:
                part = part + acc[:, col]
            if grp == groups[-1]:
                pg[:, col] = part.astype(BF16)
            else:
                acc[:, col] = part

    for x in range(1, n):
        w_copy(x).wait_send()
        f_copy(x).wait_send()
        r_copy(x).wait_send()


def body(n, queries, passages, block_list, pair_count, positive):
    rows, width = queries.shape
    r_here, pb, _ = passages.shape
    held = r_here * pb
    total = n * r_here * DISTINCT
    any_space = pl.BlockSpec(memory_space=pl.ANY)
    vmem = pl.BlockSpec(memory_space=pltpu.VMEM)
    dma = pltpu.SemaphoreType.DMA
    loss, query_grad, passage_grad = pl.pallas_call(
        functools.partial(kernel, n),
        out_shape=(
            jax.ShapeDtypeStruct((rows // BLK, BLK), F32),
            pltpu.VMEM((rows, width), BF16),
            pltpu.VMEM((held, width), BF16),
        ),
        in_specs=[any_space] * 5,
        out_specs=(vmem, vmem, vmem),
        scratch_shapes=[
            pltpu.VMEM((rows, width), BF16),
            pltpu.VMEM((held, width), BF16),
            pltpu.SMEM(block_list.shape[::-1], jnp.int32),
            pltpu.SMEM(pair_count.shape, jnp.int32),
            pltpu.VMEM((rows // BLK, BLK), jnp.int32),
            pltpu.VMEM((DISTINCT, pb), F32),
            pltpu.VMEM((n * DISTINCT, pb), F32),
            pltpu.VMEM((total, held), BF16),
            pltpu.VMEM((total, width), BF16),
            pltpu.VMEM((total, width), BF16),
            pltpu.VMEM((total, rows), F32),
            pltpu.VMEM((total, rows), BF16),
            pltpu.VMEM((total, width), BF16),
            pltpu.VMEM((total, width), BF16),
            pltpu.VMEM((held, width), F32),
            pltpu.VMEM((DISTINCT, rows), F32),
            pltpu.VMEM((DISTINCT, rows), jnp.int32),
            pltpu.VMEM((DISTINCT, rows), F32),
            pltpu.VMEM((DISTINCT, rows), F32),
            dma((5,)),
            dma,
            dma((n,)), dma((n,)), dma((n,)), dma((n,)), dma((n,)), dma((n,)),
        ],
        compiler_params=pltpu.CompilerParams(
            collective_id=0, has_side_effects=True, vmem_limit_bytes=52 * 1024 * 1024
        ),
        cost_estimate=pl.CostEstimate(
            flops=10 * rows * width * total, bytes_accessed=8 * rows * width, transcendentals=total * rows
        ),
    )(
        queries,
        passages.reshape(held, width),
        block_list.T,
        pair_count,
        positive.reshape(rows // BLK, BLK),
    )
    return loss.reshape(-1), query_grad, passage_grad.reshape(passages.shape)


def solution(mesh):
    return jax.shard_map(
        functools.partial(body, mesh.shape["blk"]),
        mesh=mesh,
        in_specs=(
            P(("groups", "blk"), None),
            P("blk", "groups", None),
            P(("groups", "blk"), None),
            P(("groups", "blk")),
            P(("groups", "blk")),
        ),
        out_specs=(P(("groups", "blk")), P(("groups", "blk"), None), P("blk", "groups", None)),
        check_vma=False,
    )
```

```python
import functools
import jax
import jax.numpy as jnp
from jax import lax
from jax.experimental import pallas as pl
from jax.experimental.pallas import tpu as pltpu
from jax.sharding import PartitionSpec as P

BLK = 128
NB = 4
DISTINCT = 8
F32 = jnp.float32
BF16 = jnp.bfloat16
NT = (((1,), (1,)), ((), ()))
TN = (((0,), (0,)), ((), ()))
TILE = 256
FAR = 3.0e38


def dot(a, b, dims=(((1,), (0,)), ((), ()))):
    return lax.dot_general(a, b, dims, preferred_element_type=F32)


def tiles(length, step):
    def over(body):
        def one(i, carry):
            body(pl.ds(pl.multiple_of(i * step, step), step))
            return carry

        lax.fori_loop(0, length // step, one, 0, unroll=True)

    return over


def kernel(
    n,
    q_hbm, p_hbm, bl_hbm, pc_hbm, pos_hbm,
    loss, qg, pg,
    q, p, bl, pc, pos, wsend, wrecv, hot, send, recv, s, g, rsend, rrecv, acc, live, tgt, m8, t8,
    in_sem, own_sem, w_s, w_r, f_s, f_r, r_s, r_r,
):
    rows, width = q.shape
    held = p.shape[0]
    pb = wsend.shape[1]
    r_here = held // pb
    mrows = r_here * DISTINCT
    qblocks = rows // BLK
    per = max(1, TILE // mrows)
    groups = list(range(n // per))
    half = n // 2
    order = [x for i in range(half) for x in (half + i, (i + 1) % half)]
    place_of = {x: i for i, x in enumerate(order)}
    me = lax.axis_index("blk")

    def peer(x):
        out, bit = me, 1
        while bit < n:
            if x & bit:
                out = out + bit - 2 * bit * (lax.rem(lax.div(me, bit), 2))
            bit *= 2
        return out

    def remote(src, dst, ss, rs, x):
        return pltpu.make_async_remote_copy(
            src_ref=src, dst_ref=dst, send_sem=ss.at[x], recv_sem=rs.at[x],
            device_id={"blk": peer(x)}, device_id_type=pl.DeviceIdType.MESH,
        )

    def slot(ref, x):
        return ref.at[pl.ds(place_of[x] * mrows, mrows)]

    def members(grp, size=per):
        return order[grp * size:(grp + 1) * size]

    def w_copy(x):
        return remote(wsend, wrecv.at[pl.ds(x * DISTINCT, DISTINCT)], w_s, w_r, x)

    def f_copy(x):
        return remote(slot(send, x), slot(recv, x), f_s, f_r, x)

    def r_copy(x):
        return remote(slot(rsend, x), slot(rrecv, x), r_s, r_r, x)

    load_q = pltpu.make_async_copy(q_hbm, q, in_sem.at[0])
    load_p = pltpu.make_async_copy(p_hbm, p, in_sem.at[1])
    small = [
        pltpu.make_async_copy(a, b, in_sem.at[2 + i])
        for i, (a, b) in enumerate(((bl_hbm, bl), (pc_hbm, pc), (pos_hbm, pos)))
    ]
    for one in small:
        one.start()
    load_p.start()
    load_q.start()
    barrier = pltpu.get_barrier_semaphore()
    for x in range(1, n):
        pl.semaphore_signal(barrier, inc=1, device_id={"blk": peer(x)}, device_id_type=pl.DeviceIdType.MESH)

    lane = lax.broadcasted_iota(jnp.int32, (DISTINCT, pb), 1)
    sub = lax.broadcasted_iota(jnp.int32, (DISTINCT, pb), 0)
    small[0].wait()
    named = lane < 0
    for k in range(qblocks):
        for j in range(NB):
            named = named | (lane == bl[j, k])
    named = named.astype(F32)
    before = (
        lax.broadcasted_iota(jnp.int32, (pb, pb), 0) < lax.broadcasted_iota(jnp.int32, (pb, pb), 1)
    ).astype(F32).astype(BF16)
    rank = dot(named.astype(BF16), before)
    mine = jnp.where(rank == sub.astype(F32), named, 0.0)
    wsend[...] = mine
    wrecv[pl.ds(0, DISTINCT), :] = mine

    pl.semaphore_wait(barrier, n - 1)
    for grp in groups:
        for x in members(grp):
            if x:
                w_copy(x).start()

    wanted = jnp.sum(mine * lane.astype(F32), axis=1, keepdims=True).astype(jnp.int32)
    small[1].wait()
    small[2].wait()
    for k in range(qblocks):
        at = pl.ds(k * BLK, BLK)
        place = jnp.broadcast_to(pos[pl.ds(k, 1), :], (DISTINCT, BLK))
        count = pc[k]
        nth = lax.shift_right_logical(place, 7)
        for _ in range(NB - 1):
            nth = jnp.where(nth >= count, nth - count, nth)
        row = place & (BLK - 1)
        is_live = jnp.zeros((DISTINCT, BLK), F32)
        target = jnp.full((DISTINCT, BLK), -1, jnp.int32)
        for j in range(NB):
            here = jnp.broadcast_to(wanted, (DISTINCT, BLK)) == bl[j, k]
            is_live = jnp.where(here & (jnp.full((DISTINCT, BLK), j, jnp.int32) < count), 1.0, is_live)
            target = jnp.where(here & (nth == j), row, target)
        live[:, at] = is_live
        tgt[:, at] = target

    load_p.wait()
    first = max(1, per // 2)
    wide = lax.broadcasted_iota(jnp.int32, (DISTINCT, held), 1)
    for grp in range(n // first):
        for x in members(grp, first):
            if x:
                w_copy(x).wait_recv()
            w = wrecv[pl.ds(x * DISTINCT, DISTINCT), :]
            w = jnp.concatenate([w] * r_here, axis=1)
            parts = [
                jnp.where((wide >= r * pb) & (wide < (r + 1) * pb), w, 0.0) for r in range(r_here)
            ]
            hot[pl.ds(place_of[x] * mrows, mrows), :] = jnp.concatenate(parts, axis=0).astype(BF16)
        at = pl.ds(grp * first * mrows, first * mrows)

        @tiles(width, TILE)
        def _(col):
            send[at, col] = dot(hot[at, :], p[:, col]).astype(BF16)

        for x in members(grp, first):
            if x:
                f_copy(x).start()
    own = pltpu.make_async_copy(slot(send, 0), slot(recv, 0), own_sem)
    own.start()
    load_q.wait()

    m8[...] = jnp.full(m8.shape, -FAR, F32)
    t8[...] = jnp.zeros(t8.shape, F32)
    for grp in groups:
        for x in members(grp):
            if x:
                f_copy(x).wait_recv()
            else:
                own.wait()
        at = pl.ds(grp * per * mrows, per * mrows)

        @tiles(rows, TILE)
        def _(col):
            part = dot(recv[at, :], q[col, :], NT)
            s[at, col] = part
            cube = part.reshape(per * r_here, DISTINCT, TILE)
            m8[:, col] = jnp.maximum(m8[:, col], jnp.max(cube, axis=0))
            total = t8[:, col]
            want = tgt[:, col]
            for i, x in enumerate(members(grp)):
                base = peer(x) * r_here
                for r in range(r_here):
                    total = total + jnp.where(want == base + r, cube[i * r_here + r], 0.0)
            t8[:, col] = total

    shown = live[...] > 0.0
    top = jnp.max(jnp.where(shown, m8[...], -FAR), axis=0, keepdims=True)
    shift = jnp.where(shown, top, FAR)
    m8[...] = shift

    def weigh(i, total):
        at = pl.ds(pl.multiple_of(i * 64, 64), 64)
        cube = s[at, :].reshape(64 // DISTINCT, DISTINCT, rows)
        e = jnp.exp(cube - m8[...][None])
        s[at, :] = e.reshape(64, rows)
        return total + jnp.sum(e, axis=0)

    total = lax.fori_loop(0, n * mrows // 64, weigh, jnp.zeros((DISTINCT, rows), F32))
    row_sum = jnp.sum(total, axis=0, keepdims=True)
    value = top + jnp.log(row_sum) - jnp.sum(t8[...], axis=0, keepdims=True)
    for k in range(qblocks):
        loss[pl.ds(k, 1), :] = value[:, k * BLK:(k + 1) * BLK]
    t8[...] = jnp.broadcast_to(1.0 / row_sum, t8.shape)

    last = max(1, per // 2)
    for grp in range(n // last):
        for x in members(grp, last):
            base = peer(x) * r_here
            at = pl.ds(place_of[x] * mrows, mrows)
            cube = s[at, :].reshape(r_here, DISTINCT, rows)
            which = base + lax.broadcasted_iota(jnp.int32, cube.shape, 0)
            one = jnp.where(tgt[...][None] == which, 1.0, 0.0)
            g[at, :] = (cube * t8[...][None] - one).reshape(mrows, rows).astype(BF16)
        at = pl.ds(grp * last * mrows, last * mrows)

        @tiles(width, TILE)
        def _(col):
            rsend[at, col] = dot(g[at, :], q[:, col]).astype(BF16)

        for x in members(grp, last):
            if x:
                r_copy(x).start()

    @tiles(width, TILE)
    def _(col):
        qg[:, col] = dot(g[...], recv[:, col], TN).astype(BF16)


    own = pltpu.make_async_copy(slot(rsend, 0), slot(rrecv, 0), own_sem)
    own.start()
    for grp in groups:
        for x in members(grp):
            if x:
                r_copy(x).wait_recv()
            else:
                own.wait()
        at = pl.ds(grp * per * mrows, per * mrows)

        @tiles(width, TILE)
        def _(col):
            part = dot(hot[at, :], rrecv[at, col], TN)
            if grp != groups[0]:
                part = part + acc[:, col]
            if grp == groups[-1]:
                pg[:, col] = part.astype(BF16)
            else:
                acc[:, col] = part

    for x in range(1, n):
        w_copy(x).wait_send()
        f_copy(x).wait_send()
        r_copy(x).wait_send()


def body(n, queries, passages, block_list, pair_count, positive):
    rows, width = queries.shape
    r_here, pb, _ = passages.shape
    held = r_here * pb
    total = n * r_here * DISTINCT
    any_space = pl.BlockSpec(memory_space=pl.ANY)
    vmem = pl.BlockSpec(memory_space=pltpu.VMEM)
    dma = pltpu.SemaphoreType.DMA
    loss, query_grad, passage_grad = pl.pallas_call(
        functools.partial(kernel, n),
        out_shape=(
            jax.ShapeDtypeStruct((rows // BLK, BLK), F32),
            pltpu.VMEM((rows, width), BF16),
            pltpu.VMEM((held, width), BF16),
        ),
        in_specs=[any_space] * 5,
        out_specs=(vmem, vmem, vmem),
        scratch_shapes=[
            pltpu.VMEM((rows, width), BF16),
            pltpu.VMEM((held, width), BF16),
            pltpu.SMEM(block_list.shape[::-1], jnp.int32),
            pltpu.SMEM(pair_count.shape, jnp.int32),
            pltpu.VMEM((rows // BLK, BLK), jnp.int32),
            pltpu.VMEM((DISTINCT, pb), F32),
            pltpu.VMEM((n * DISTINCT, pb), F32),
            pltpu.VMEM((total, held), BF16),
            pltpu.VMEM((total, width), BF16),
            pltpu.VMEM((total, width), BF16),
            pltpu.VMEM((total, rows), F32),
            pltpu.VMEM((total, rows), BF16),
            pltpu.VMEM((total, width), BF16),
            pltpu.VMEM((total, width), BF16),
            pltpu.VMEM((held, width), F32),
            pltpu.VMEM((DISTINCT, rows), F32),
            pltpu.VMEM((DISTINCT, rows), jnp.int32),
            pltpu.VMEM((DISTINCT, rows), F32),
            pltpu.VMEM((DISTINCT, rows), F32),
            dma((5,)),
            dma,
            dma((n,)), dma((n,)), dma((n,)), dma((n,)), dma((n,)), dma((n,)),
        ],
        compiler_params=pltpu.CompilerParams(
            collective_id=0, has_side_effects=True, vmem_limit_bytes=52 * 1024 * 1024
        ),
        cost_estimate=pl.CostEstimate(
            flops=10 * rows * width * total, bytes_accessed=8 * rows * width, transcendentals=total * rows
        ),
    )(
        queries,
        passages.reshape(held, width),
        block_list.T,
        pair_count,
        positive.reshape(rows // BLK, BLK),
    )
    return loss.reshape(-1), query_grad, passage_grad.reshape(passages.shape)


def solution(mesh):
    return jax.shard_map(
        functools.partial(body, mesh.shape["blk"]),
        mesh=mesh,
        in_specs=(
            P(("groups", "blk"), None),
            P("blk", "groups", None),
            P(("groups", "blk"), None),
            P(("groups", "blk")),
            P(("groups", "blk")),
        ),
        out_specs=(P(("groups", "blk")), P(("groups", "blk"), None), P("blk", "groups", None)),
        check_vma=False,
    )
```
